128 devices in a mesh: dp: 8 (over x, core), tensor: 16 (over z, y).
Axes of the slice: x: 4, y: 4, z: 4, core: 2. Of those that a mesh axis runs over, the one named last changes fastest.
Arguments:
- tokens: bfloat16 [512, 8192], P(None, 'dp'), may hold values from -6 to 6
- gate_codes: int32 [8192, 32768], P('dp', 'tensor'), may hold values from 0 to 15
- up_codes: int32 [8192, 32768], P('dp', 'tensor'), may hold values from 0 to 15
- down_codes: int32 [32768, 8192], P('tensor', 'dp'), may hold values from 0 to 15
- gate_scale: int32 [32768], P('tensor'), may hold values from 8 to 39
- up_scale: int32 [32768], P('tensor'), may hold values from 8 to 39
- down_scale: int32 [8192], P('dp'), may hold values from 8 to 39
Outputs:
- mixed: bfloat16 [512, 8192], P('tensor', 'dp')
The draws below stay inside these ranges and needn't reach their ends.
All inputs are finite; a program needn't handle non-finite values.
Results may differ from the reference program's by a relative error of at most 0.035.
Values may be sent and summed in bfloat16 or wider, within the bound.
A program may use at most 128 MiB of HBM per device.

```python
import math
import jax
import jax.numpy as jnp

D = 8192
FF = 32768
TOKENS = 512
N_DP = 8


def set_ends(drawn, stream_key, low, top_value):
    longest = drawn.shape.index(max(drawn.shape))
    spots = []
    for shift in (0, 1):
        where = [jax.random.randint(jax.random.fold_in(stream_key, axis), (), 0, length) for axis, length in enumerate(drawn.shape)]
        where[longest] = (where[longest] + shift) % drawn.shape[longest]
        spots.append(tuple(where))
    return drawn.at[spots[0]].set(low).at[spots[1]].set(top_value)


def strengthened(drawn, own_key, source, target, parts, factor):
    owner, partner = [(jnp.arange(drawn.shape[dim]) // (drawn.shape[dim] // parts)).reshape([-1 if axis == dim else 1 for axis in range(drawn.ndim)]) for dim in (source, target)]
    chosen = jax.random.permutation(own_key, parts)[partner]
    strong = (owner == chosen) | (owner == (partner + parts // 2) % parts)
    return jnp.where(strong, factor * drawn, drawn)


def block_scale(own_key, dims, shards, low, largest):
    def one(axis_at, parts):
        steps = jax.random.uniform(jax.random.fold_in(jax.random.fold_in(own_key, 6), axis_at), (parts,), jnp.float32, low / len(shards), largest / len(shards))
        return jnp.repeat(jnp.exp(steps), dims[axis_at] // parts).reshape((-1,) + (1,) * (len(dims) - axis_at - 1))

    level = one(*shards[0])
    for cut in shards[1:]:
        level = level * one(*cut)
    return level


def gaussian_with(key, extent, scale, bound, pieces, heavy, dtype=jnp.bfloat16):
    values = scale * jax.random.normal(key, extent, jnp.float32)
    if pieces:
        values = values * block_scale(key, extent, pieces, -0.22, 0.18)
    return jnp.clip(strengthened(values, jax.random.fold_in(key, 3), *heavy), -bound, bound).astype(dtype)


def setup_inputs(seed: int = 0) -> dict:
    key_of = jax.random.split(jax.random.key(seed), 8)
    tokens = gaussian_with(key_of[0], (TOKENS, D), 1.0, 6.0, ((1, 8),), (1, 0, 8, 2.0))
    gate_codes = set_ends(jax.random.randint(key_of[1], (D, FF), 0, 16), jax.random.fold_in(key_of[1], 1), 0, 15).astype(jnp.int32)
    up_codes = set_ends(jax.random.randint(key_of[2], (D, FF), 0, 16), jax.random.fold_in(key_of[2], 1), 0, 15).astype(jnp.int32)
    down_codes = set_ends(jax.random.randint(key_of[3], (FF, D), 0, 16), jax.random.fold_in(key_of[3], 1), 0, 15).astype(jnp.int32)
    gate_scale = set_ends(jax.random.randint(key_of[4], (FF,), 8, 40), jax.random.fold_in(key_of[4], 1), 8, 39).astype(jnp.int32)
    up_scale = set_ends(jax.random.randint(key_of[5], (FF,), 8, 40), jax.random.fold_in(key_of[5], 1), 8, 39).astype(jnp.int32)
    down_scale = set_ends(jax.random.randint(key_of[6], (D,), 8, 40), jax.random.fold_in(key_of[6], 1), 8, 39).astype(jnp.int32)
    return dict(tokens=tokens, gate_codes=gate_codes, up_codes=up_codes, down_codes=down_codes, gate_scale=gate_scale, up_scale=up_scale, down_scale=down_scale)


def walsh_transform(values):
    row_total, unit_total = values.shape
    stride = 1
    while stride < unit_total:
        shaped = values.reshape(row_total, unit_total // (2 * stride), 2, stride)
        first_half = shaped[:, :, 0, :]
        second_half = shaped[:, :, 1, :]
        values = jnp.stack([first_half + second_half, first_half - second_half], axis=2).reshape(row_total, unit_total)
        stride = stride * 2
    return values

def reference(tokens, gate_codes, up_codes, down_codes, gate_scale, up_scale, down_scale):
    block_width = D // N_DP
    gate_total = jnp.zeros((TOKENS, FF), jnp.float32)
    up_total = jnp.zeros((TOKENS, FF), jnp.float32)
    for block_index in range(N_DP):
        first_col = block_index * block_width
        feature_block = tokens[:, first_col:first_col + block_width]
        gate_block = (gate_codes[first_col:first_col + block_width, :] - 8).astype(jnp.bfloat16)
        up_block = (up_codes[first_col:first_col + block_width, :] - 8).astype(jnp.bfloat16)
        gate_piece = jnp.dot(feature_block, gate_block, preferred_element_type=jnp.float32).astype(jnp.bfloat16)
        up_piece = jnp.dot(feature_block, up_block, preferred_element_type=jnp.float32).astype(jnp.bfloat16)
        gate_total = gate_total + gate_piece.astype(jnp.float32)
        up_total = up_total + up_piece.astype(jnp.float32)
    gate_value = gate_total * (gate_scale.astype(jnp.float32) / (128.0 * math.sqrt(D)))
    up_value = up_total * (up_scale.astype(jnp.float32) / (128.0 * math.sqrt(D)))
    hidden = (jax.nn.silu(gate_value) * up_value).astype(jnp.bfloat16)
    rotated = (walsh_transform(hidden.astype(jnp.float32)) / math.sqrt(FF)).astype(jnp.bfloat16)
    down_matrix = (down_codes - 8).astype(jnp.bfloat16)
    projected = jnp.dot(rotated, down_matrix, preferred_element_type=jnp.float32)
    return (projected * (down_scale.astype(jnp.float32) / (64.0 * math.sqrt(FF)))).astype(jnp.bfloat16)
```

```python
import functools
import math

import jax
import jax.numpy as jnp
from jax import lax
from jax.experimental import pallas as pl
from jax.experimental.pallas import tpu as pltpu
from jax.sharding import PartitionSpec as P

D = 8192
FF = 32768
TOKENS = 512
NX = 4
OWN = TOKENS // (2 * NX)
SUB = OWN // 2
TILES = 8
LAG_B, LAG_C, LAG_D = 1, 2, 3
MESH = pl.DeviceIdType.MESH
F32 = jnp.float32
BF16 = jnp.bfloat16


def remote(src, dst, send_sem, recv_sem, device):
    return pltpu.make_async_remote_copy(
        src_ref=src,
        dst_ref=dst,
        send_sem=send_sem,
        recv_sem=recv_sem,
        device_id=device,
        device_id_type=MESH,
    )


def walsh(parts):
    stride = 1
    while stride < len(parts):
        done = list(parts)
        for i in range(len(parts)):
            if i & stride == 0:
                done[i] = parts[i] + parts[i + stride]
                done[i + stride] = parts[i] - parts[i + stride]
        parts = done
        stride *= 2
    return parts


def signs(size):
    rows = lax.broadcasted_iota(jnp.int32, (size, size), 0)
    cols = lax.broadcasted_iota(jnp.int32, (size, size), 1)
    bits = jnp.bitwise_and(rows, cols)
    for shift in (8, 4, 2, 1):
        bits = jnp.bitwise_xor(bits, jnp.right_shift(bits, shift))
    return (1 - 2 * jnp.bitwise_and(bits, 1)).astype(F32).astype(BF16)


def kernel(
    nt, ff,
    tok_hbm, gate_hbm, up_hbm, down_hbm, gs_ref, us_ref, ds_ref,
    out_ref,
    tok_in, tok, codes, down_codes, w, wd, had,
    core_out, core_in, acc, x_out, x_in,
    rot, z, a, r, y, part, gathered,
    tok_sem, code_sem, down_sem,
    core_ssem, core_rsem, x_ssem, x_rsem,
    z_ssem, z_rsem, r_ssem, r_rsem, ag_ssem, ag_rsem, rs_ssem, rs_rsem,
):
    dp = lax.axis_index("dp")
    me = lax.axis_index("tensor")
    x = dp // 2
    c = dp % 2
    right = lax.rem(x + 1, NX)
    left = lax.rem(x + NX - 1, NX)
    across = lax.rem(x + 2, NX)
    dev_core = (x * 2 + 1 - c, me)
    dev_right = (right * 2 + c, me)
    dev_left = (left * 2 + c, me)
    units = gate_hbm.shape[1]
    wide = units // TILES
    depth = gate_hbm.shape[0]
    d_rows = down_hbm.shape[0] // TILES
    group = TOKENS // (NX * nt)
    piece = units // nt

    def peer(k):
        return lax.rem(me + k, nt)

    barrier = pltpu.get_barrier_semaphore()
    for device in (dev_core, dev_right, dev_left):
        pl.semaphore_signal(barrier, inc=1, device_id=device, device_id_type=MESH)

    def greet(k, carry):
        pl.semaphore_signal(barrier, inc=1, device_id=(dp, peer(k)), device_id_type=MESH)
        return carry

    lax.fori_loop(1, nt, greet, 0)

    tok_copy = pltpu.make_async_copy(tok_hbm, tok_in, tok_sem.at[0])
    tok_copy.start()

    def gate_copy(t):
        return pltpu.make_async_copy(
            gate_hbm.at[:, pl.ds(pl.multiple_of(t * wide, wide), wide)], codes.at[t, 0], code_sem.at[t, 0]
        )

    def up_copy(t):
        return pltpu.make_async_copy(
            up_hbm.at[:, pl.ds(pl.multiple_of(t * wide, wide), wide)], codes.at[t, 1], code_sem.at[t, 1]
        )

    def down_copy(t):
        rows = pl.ds(pl.multiple_of(t * d_rows, d_rows), d_rows)
        return pltpu.make_async_copy(down_hbm.at[rows, :], down_codes.at[rows, :], down_sem.at[t])

    def start_codes(t, carry):
        gate_copy(t).start()
        up_copy(t).start()
        return carry

    def start_down(t, carry):
        down_copy(t).start()
        return carry

    lax.fori_loop(0, TILES, start_codes, 0)
    lax.fori_loop(0, TILES, start_down, 0)

    had[...] = signs(wide)

    tok_copy.wait()
    half_groups = nt // 2
    for half in range(2):
        for chip in range(NX):
            rows = []
            for j in range(half_groups):
                first = (half * half_groups + j) * (TOKENS // nt) + chip * group
                rows.append(tok_in[first // 16 * 16 : first // 16 * 16 + max(16, group), :].astype(F32)[
                    first % 16 : first % 16 + group])
            start = half * (TOKENS // 2) + chip * OWN
            tok[start : start + OWN, :] = jnp.concatenate(rows, axis=0).astype(BF16)

    other_rows = pl.ds(pl.multiple_of((1 - c) * (TOKENS // 2), TOKENS // 2), TOKENS // 2)
    own_rows = pl.ds(pl.multiple_of(c * (TOKENS // 2), TOKENS // 2), TOKENS // 2)

    def rows_of(chip, half):
        return pl.ds(pl.multiple_of(chip * OWN + half * SUB, SUB), SUB)

    def core_copy(t):
        return remote(core_out.at[t], core_in.at[t], core_ssem.at[t], core_rsem.at[t], dev_core)

    def x_copy(t, way, kind):
        return remote(
            x_out.at[t, way, kind], x_in.at[t, way, kind], x_ssem.at[t, way, kind], x_rsem.at[t, way, kind],
            dev_right if way == 0 else dev_left,
        )

    def stage_a(t):
        gate_copy(t).wait()
        up_copy(t).wait()
        w[:, :wide] = (codes[t, 0] - 8).astype(F32).astype(BF16)
        w[:, wide:] = (codes[t, 1] - 8).astype(F32).astype(BF16)
        core_out[t] = jnp.dot(tok[other_rows, :], w[...], preferred_element_type=F32).astype(BF16)

        @pl.when(t == 0)
        def _():
            pl.semaphore_wait(barrier, 3 + nt - 1)

        core_copy(t).start()
        acc[t] = jnp.dot(tok[own_rows, :], w[...], preferred_element_type=F32)
        down_copy(t).wait()
        rows = pl.ds(pl.multiple_of(t * d_rows, d_rows), d_rows)
        wd[rows, :] = (down_codes[rows, :] - 8).astype(F32).astype(BF16)

    def stage_b(t):
        core_copy(t).wait_recv()

        def both(rows):
            return acc[t, rows, :] + core_in[t, rows, :].astype(F32)

        x_out[t, 0, 0] = both(rows_of(across, 0)).astype(BF16)
        x_copy(t, 0, 0).start()
        x_out[t, 1, 0] = both(rows_of(across, 1)).astype(BF16)
        x_copy(t, 1, 0).start()
        x_out[t, 0, 1] = both(rows_of(right, 1)).astype(BF16)
        x_copy(t, 0, 1).start()
        x_out[t, 1, 1] = both(rows_of(left, 0)).astype(BF16)
        x_copy(t, 1, 1).start()
        for rows in (rows_of(right, 0), rows_of(left, 1), rows_of(x, 0), rows_of(x, 1)):
            acc[t, rows, :] = both(rows)

    def stage_c(t):
        x_copy(t, 0, 0).wait_recv()
        x_out[t, 0, 2] = (acc[t, rows_of(right, 0), :] + x_in[t, 0, 0].astype(F32)).astype(BF16)
        x_copy(t, 0, 2).start()
        x_copy(t, 1, 0).wait_recv()
        x_out[t, 1, 2] = (acc[t, rows_of(left, 1), :] + x_in[t, 1, 0].astype(F32)).astype(BF16)
        x_copy(t, 1, 2).start()

    def stage_d(t):
        for way in range(2):
            for kind in (1, 2):
                x_copy(t, way, kind).wait_recv()
        low = acc[t, rows_of(x, 0), :] + x_in[t, 0, 2].astype(F32) + x_in[t, 1, 1].astype(F32)
        high = acc[t, rows_of(x, 1), :] + x_in[t, 0, 1].astype(F32) + x_in[t, 1, 2].astype(F32)
        total = jnp.concatenate([low, high], axis=0)
        unit = 1.0 / (128.0 * math.sqrt(D))
        gate = total[:, :wide] * (gs_ref[t].astype(F32) * unit)
        up = total[:, wide:] * (us_ref[t].astype(F32) * unit)
        hidden = (gate / (1.0 + jnp.exp(-gate)) * up).astype(BF16)
        rot[t] = jnp.dot(hidden, had[...], preferred_element_type=F32)

    def step(s, carry):
        pl.when(s < TILES)(lambda: stage_a(s))
        pl.when(jnp.logical_and(s >= LAG_B, s < TILES + LAG_B))(lambda: stage_b(s - LAG_B))
        pl.when(jnp.logical_and(s >= LAG_C, s < TILES + LAG_C))(lambda: stage_c(s - LAG_C))
        pl.when(s >= LAG_D)(lambda: stage_d(s - LAG_D))
        return carry

    lax.fori_loop(0, TILES + LAG_D, step, 0)

    for rows in range(0, OWN, 16):
        mixed = walsh([rot[t, rows : rows + 16, :] for t in range(TILES)])
        flat = jnp.concatenate(mixed, axis=1).astype(BF16)
        for j in range(nt):
            z[j, rows : rows + 16, :] = flat[:, j * piece : (j + 1) * piece]

    def z_copy(j, slot):
        return remote(z.at[j], a.at[slot], z_ssem.at[j], z_rsem.at[slot], (dp, j))

    def z_send(k, carry):
        z_copy(peer(k), me).start()
        return carry

    def z_wait(k, carry):
        z_copy(me, peer(k)).wait_recv()
        return carry

    lax.fori_loop(1, nt, z_send, 0)
    a[me] = z[me]
    lax.fori_loop(1, nt, z_wait, 0)

    for rows in range(0, OWN, 16):
        mixed = walsh([a[i, rows : rows + 16, :].astype(F32) for i in range(nt)])
        for j in range(nt):
            r[j, rows : rows + 16, :] = (mixed[j] * (1.0 / math.sqrt(ff))).astype(BF16)

    my_rows = pl.ds(pl.multiple_of(c * OWN, OWN), OWN)
    other_core = pl.ds(pl.multiple_of((1 - c) * OWN, OWN), OWN)

    def r_copy(j, slot):
        cols = pl.ds(pl.multiple_of(slot * piece, piece), piece)
        return remote(r.at[j], y.at[x, my_rows, cols], r_ssem.at[j], r_rsem.at[slot], (dp, j))

    def r_send(k, carry):
        r_copy(peer(k), me).start()
        return carry

    def r_wait(k, carry):
        r_copy(me, peer(k)).wait_recv()
        return carry

    lax.fori_loop(1, nt, r_send, 0)
    y[x, my_rows, pl.ds(pl.multiple_of(me * piece, piece), piece)] = r[me]
    lax.fori_loop(1, nt, r_wait, 0)

    half_rows = [pl.ds(pl.multiple_of(c * OWN + h * SUB, SUB), SUB) for h in range(2)]

    def ag(sem, chip, rows, device):
        return remote(y.at[chip, rows, :], y.at[chip, rows, :], ag_ssem.at[sem], ag_rsem.at[sem], device)

    ag(0, x, my_rows, dev_right).start()
    ag(1, x, my_rows, dev_left).start()
    ag(2, x, my_rows, dev_core).start()

    def rs_copy(chip, j, slot):
        return remote(
            part.at[chip, j], gathered.at[chip, slot], rs_ssem.at[chip, j], rs_rsem.at[chip, slot], (dp, j)
        )

    def down(chip):
        result = jnp.dot(y[chip], wd[...], preferred_element_type=F32)
        middle = result.shape[1] // 2
        for j in range(nt):
            rows = result[j * group : (j + 1) * group]
            part[chip, j] = jnp.concatenate([rows[:, :middle], rows[:, middle:]], axis=0).astype(BF16)

        def send(k, carry):
            rs_copy(chip, peer(k), me).start()
            return carry

        lax.fori_loop(1, nt, send, 0)
        gathered[chip, me] = part[chip, me]

    ag(2, x, other_core, dev_core).wait_recv()
    down(x)

    ag(0, left, my_rows, dev_right).wait_recv()
    ag(3, left, half_rows[0], dev_right).start()
    ag(4, left, my_rows, dev_core).start()
    ag(1, right, my_rows, dev_left).wait_recv()
    ag(5, right, half_rows[1], dev_left).start()
    ag(6, right, my_rows, dev_core).start()

    ag(4, left, other_core, dev_core).wait_recv()
    down(left)
    ag(6, right, other_core, dev_core).wait_recv()
    down(right)

    ag(3, across, half_rows[0], dev_right).wait_recv()
    ag(7, across, half_rows[0], dev_core).start()
    ag(5, across, half_rows[1], dev_left).wait_recv()
    ag(8, across, half_rows[1], dev_core).start()
    other_half = [pl.ds(pl.multiple_of((1 - c) * OWN + h * SUB, SUB), SUB) for h in range(2)]
    ag(7, across, other_half[0], dev_core).wait_recv()
    ag(8, across, other_half[1], dev_core).wait_recv()
    down(across)

    def rs_wait(n, carry):
        rs_copy(n // (nt - 1), me, peer(n % (nt - 1) + 1)).wait_recv()
        return carry

    lax.fori_loop(0, NX * (nt - 1), rs_wait, 0)
    scale = ds_ref[...].astype(F32) * (1.0 / (64.0 * math.sqrt(ff)))
    blocks = []
    for chip in range(NX):
        total = gathered[chip, 0].astype(F32)
        for i in range(1, nt):
            total = total + gathered[chip, i].astype(F32)
        blocks.append(jnp.concatenate([total[:group], total[group:]], axis=1) * scale)
    out_ref[...] = jnp.concatenate(blocks, axis=0).astype(BF16)

    def core_done(t, carry):
        core_copy(t).wait_send()
        for way in range(2):
            for kind in range(3):
                x_copy(t, way, kind).wait_send()
        return carry

    lax.fori_loop(0, TILES, core_done, 0)

    def peers_done(k, carry):
        z_copy(peer(k), me).wait_send()
        r_copy(peer(k), me).wait_send()
        return carry

    lax.fori_loop(1, nt, peers_done, 0)

    def rs_done(n, carry):
        rs_copy(n // (nt - 1), peer(n % (nt - 1) + 1), me).wait_send()
        return carry

    lax.fori_loop(0, NX * (nt - 1), rs_done, 0)
    ag(0, x, my_rows, dev_right).wait_send()
    ag(1, x, my_rows, dev_left).wait_send()
    ag(2, x, my_rows, dev_core).wait_send()
    ag(3, left, half_rows[0], dev_right).wait_send()
    ag(4, left, my_rows, dev_core).wait_send()
    ag(5, right, half_rows[1], dev_left).wait_send()
    ag(6, right, my_rows, dev_core).wait_send()
    ag(7, across, half_rows[0], dev_core).wait_send()
    ag(8, across, half_rows[1], dev_core).wait_send()


def body(tokens, gate_codes, up_codes, down_codes, gate_scale, up_scale, down_scale):
    nt = lax.axis_size("tensor")
    depth, units = gate_codes.shape
    width = down_codes.shape[1]
    wide = units // TILES
    piece = units // nt
    group = TOKENS // (NX * nt)
    dma = pltpu.SemaphoreType.DMA
    any_space = pl.BlockSpec(memory_space=pl.ANY)
    vmem = pl.BlockSpec(memory_space=pltpu.VMEM)
    return pl.pallas_call(
        functools.partial(kernel, nt, units * nt),
        out_shape=jax.ShapeDtypeStruct((TOKENS // nt, width), BF16),
        in_specs=[any_space] * 4 + [vmem] * 3,
        out_specs=vmem,
        scratch_shapes=[
            pltpu.VMEM((TOKENS, depth), BF16),
            pltpu.VMEM((TOKENS, depth), BF16),
            pltpu.VMEM((TILES, 2, depth, wide), jnp.int32),
            pltpu.VMEM((units, width), jnp.int32),
            pltpu.VMEM((depth, 2 * wide), BF16),
            pltpu.VMEM((units, width), BF16),
            pltpu.VMEM((wide, wide), BF16),
            pltpu.VMEM((TILES, TOKENS // 2, 2 * wide), BF16),
            pltpu.VMEM((TILES, TOKENS // 2, 2 * wide), BF16),
            pltpu.VMEM((TILES, TOKENS // 2, 2 * wide), F32),
            pltpu.VMEM((TILES, 2, 3, SUB, 2 * wide), BF16),
            pltpu.VMEM((TILES, 2, 3, SUB, 2 * wide), BF16),
            pltpu.VMEM((TILES, OWN, wide), F32),
            pltpu.VMEM((nt, OWN, piece), BF16),
            pltpu.VMEM((nt, OWN, piece), BF16),
            pltpu.VMEM((nt, OWN, piece), BF16),
            pltpu.VMEM((NX, 2 * OWN, units), BF16),
            pltpu.VMEM((NX, nt, 2 * group, width // 2), BF16),
            pltpu.VMEM((NX, nt, 2 * group, width // 2), BF16),
            dma((1,)),
            dma((TILES, 2)),
            dma((TILES,)),
            dma((TILES,)),
            dma((TILES,)),
            dma((TILES, 2, 3)),
            dma((TILES, 2, 3)),
            dma((nt,)),
            dma((nt,)),
            dma((nt,)),
            dma((nt,)),
            dma((9,)),
            dma((9,)),
            dma((NX, nt)),
            dma((NX, nt)),
        ],
        compiler_params=pltpu.CompilerParams(
            collective_id=0, has_side_effects=True, vmem_limit_bytes=56 * 1024 * 1024
        ),
        cost_estimate=pl.CostEstimate(
            flops=2 * TOKENS * depth * 3 * units, bytes_accessed=12 * depth * units, transcendentals=OWN * units
        ),
    )(
        tokens, gate_codes, up_codes, down_codes,
        gate_scale.reshape(TILES, 1, wide), up_scale.reshape(TILES, 1, wide), down_scale.reshape(1, width),
    )


def solution(mesh):
    in_specs = (
        P(None, "dp"),
        P("dp", "tensor"),
        P("dp", "tensor"),
        P("tensor", "dp"),
        P("tensor"),
        P("tensor"),
        P("dp"),
    )
    return jax.shard_map(body, mesh=mesh, in_specs=in_specs, out_specs=P("tensor", "dp"), check_vma=False)
```

```python
import functools
import math

import jax
import jax.numpy as jnp
from jax import lax
from jax.experimental import pallas as pl
from jax.experimental.pallas import tpu as pltpu
from jax.sharding import PartitionSpec as P

D = 8192
FF = 32768
TOKENS = 512
NX = 4
OWN = TOKENS // (2 * NX)
SUB = OWN // 2
TILES = 8
LAG_B, LAG_C, LAG_D = 1, 3, 6
MESH = pl.DeviceIdType.MESH
F32 = jnp.float32
BF16 = jnp.bfloat16


def remote(src, dst, send_sem, recv_sem, device):
    return pltpu.make_async_remote_copy(
        src_ref=src,
        dst_ref=dst,
        send_sem=send_sem,
        recv_sem=recv_sem,
        device_id=device,
        device_id_type=MESH,
    )


def walsh(parts):
    stride = 1
    while stride < len(parts):
        done = list(parts)
        for i in range(len(parts)):
            if i & stride == 0:
                done[i] = parts[i] + parts[i + stride]
                done[i + stride] = parts[i] - parts[i + stride]
        parts = done
        stride *= 2
    return parts


def signs(size):
    rows = lax.broadcasted_iota(jnp.int32, (size, size), 0)
    cols = lax.broadcasted_iota(jnp.int32, (size, size), 1)
    bits = jnp.bitwise_and(rows, cols)
    for shift in (8, 4, 2, 1):
        bits = jnp.bitwise_xor(bits, jnp.right_shift(bits, shift))
    return (1 - 2 * jnp.bitwise_and(bits, 1)).astype(F32).astype(BF16)


def kernel(
    nt, ff,
    tok_hbm, gate_hbm, up_hbm, down_hbm, gs_ref, us_ref, ds_ref,
    out_ref,
    tok_in, tok, codes, down_codes, w, wd, had,
    core_out, core_in, acc, x_out, x_in,
    rot, z, a, r, y, part, gathered,
    tok_sem, code_sem, down_sem,
    core_ssem, core_rsem, x_ssem, x_rsem,
    z_ssem, z_rsem, r_ssem, r_rsem, ag_ssem, ag_rsem, rs_ssem, rs_rsem, plane_sem,
):
    dp = lax.axis_index("dp")
    me = lax.axis_index("tensor")
    x = dp // 2
    c = dp % 2
    right = lax.rem(x + 1, NX)
    left = lax.rem(x + NX - 1, NX)
    across = lax.rem(x + 2, NX)
    dev_core = (x * 2 + 1 - c, me)
    dev_right = (right * 2 + c, me)
    dev_left = (left * 2 + c, me)
    units = gate_hbm.shape[1]
    wide = units // TILES
    depth = gate_hbm.shape[0]
    d_rows = down_hbm.shape[0] // TILES
    group = TOKENS // (NX * nt)
    piece = units // nt

    def peer(k):
        return lax.rem(me + k, nt)

    tok_copy = pltpu.make_async_copy(tok_hbm, tok_in, tok_sem.at[0])
    tok_copy.start()

    def gate_copy(t):
        return pltpu.make_async_copy(
            gate_hbm.at[:, pl.ds(pl.multiple_of(t * wide, wide), wide)], codes.at[t, 0], code_sem.at[t, 0]
        )

    def up_copy(t):
        return pltpu.make_async_copy(
            up_hbm.at[:, pl.ds(pl.multiple_of(t * wide, wide), wide)], codes.at[t, 1], code_sem.at[t, 1]
        )

    def down_copy(t):
        rows = pl.ds(pl.multiple_of(t * d_rows, d_rows), d_rows)
        return pltpu.make_async_copy(down_hbm.at[rows, :], down_codes.at[rows, :], down_sem.at[t])

    def start_codes(t, carry):
        gate_copy(t).start()
        up_copy(t).start()
        return carry

    def start_down(t, carry):
        down_copy(t).start()
        return carry

    lax.fori_loop(0, TILES, start_codes, 0)
    lax.fori_loop(0, TILES, start_down, 0)

    barrier = pltpu.get_barrier_semaphore()
    side = math.isqrt(nt)
    row, col = me // side, me % side
    along_y = [(dp, row * side + lax.rem(col + k, side)) for k in range(1, side)]
    along_z = [(dp, lax.rem(row + k, side) * side + col) for k in range(1, side)]
    greeted = [dev_core, dev_right, dev_left] + along_y + along_z
    for device in greeted:
        pl.semaphore_signal(barrier, inc=1, device_id=device, device_id_type=MESH)

    had[...] = signs(wide)

    tok_copy.wait()
    half_groups = nt // 2
    for half in range(2):
        for chip in range(NX):
            rows = []
            for j in range(half_groups):
                first = (half * half_groups + j) * (TOKENS // nt) + chip * group
                rows.append(tok_in[first // 16 * 16 : first // 16 * 16 + max(16, group), :].astype(F32)[
                    first % 16 : first % 16 + group])
            start = half * (TOKENS // 2) + chip * OWN
            tok[start : start + OWN, :] = jnp.concatenate(rows, axis=0).astype(BF16)

    other_rows = pl.ds(pl.multiple_of((1 - c) * (TOKENS // 2), TOKENS // 2), TOKENS // 2)
    own_rows = pl.ds(pl.multiple_of(c * (TOKENS // 2), TOKENS // 2), TOKENS // 2)

    def rows_of(chip, half):
        return pl.ds(pl.multiple_of(chip * OWN + half * SUB, SUB), SUB)

    def core_copy(t):
        return remote(core_out.at[t], core_in.at[t], core_ssem.at[t], core_rsem.at[t], dev_core)

    def x_copy(t, way, kind):
        return remote(
            x_out.at[t, way, kind], x_in.at[t, way, kind], x_ssem.at[t, way, kind], x_rsem.at[t, way, kind],
            dev_right if way == 0 else dev_left,
        )

    def stage_a(t):
        gate_copy(t).wait()
        up_copy(t).wait()
        w[:, :wide] = (codes[t, 0] - 8).astype(F32).astype(BF16)
        w[:, wide:] = (codes[t, 1] - 8).astype(F32).astype(BF16)
        core_out[t] = jnp.dot(tok[other_rows, :], w[...], preferred_element_type=F32).astype(BF16)

        @pl.when(t == 0)
        def _():
            pl.semaphore_wait(barrier, len(greeted))
            for device in along_z:
                pl.semaphore_signal(plane_sem, inc=1, device_id=device, device_id_type=MESH)

        core_copy(t).start()
        acc[t] = jnp.dot(tok[own_rows, :], w[...], preferred_element_type=F32)
        down_copy(t).wait()
        rows = pl.ds(pl.multiple_of(t * d_rows, d_rows), d_rows)
        wd[rows, :] = (down_codes[rows, :] - 8).astype(F32).astype(BF16)

    def stage_b(t):
        core_copy(t).wait_recv()

        def both(rows):
            return acc[t, rows, :] + core_in[t, rows, :].astype(F32)

        x_out[t, 0, 0] = both(rows_of(across, 0)).astype(BF16)
        x_copy(t, 0, 0).start()
        x_out[t, 1, 0] = both(rows_of(across, 1)).astype(BF16)
        x_copy(t, 1, 0).start()
        x_out[t, 0, 1] = both(rows_of(right, 1)).astype(BF16)
        x_copy(t, 0, 1).start()
        x_out[t, 1, 1] = both(rows_of(left, 0)).astype(BF16)
        x_copy(t, 1, 1).start()
        for rows in (rows_of(right, 0), rows_of(left, 1), rows_of(x, 0), rows_of(x, 1)):
            acc[t, rows, :] = both(rows)

    def stage_c(t):
        x_copy(t, 0, 0).wait_recv()
        x_out[t, 0, 2] = (acc[t, rows_of(right, 0), :] + x_in[t, 0, 0].astype(F32)).astype(BF16)
        x_copy(t, 0, 2).start()
        x_copy(t, 1, 0).wait_recv()
        x_out[t, 1, 2] = (acc[t, rows_of(left, 1), :] + x_in[t, 1, 0].astype(F32)).astype(BF16)
        x_copy(t, 1, 2).start()

    def stage_d(t):
        for way in range(2):
            for kind in (1, 2):
                x_copy(t, way, kind).wait_recv()
        low = acc[t, rows_of(x, 0), :] + x_in[t, 0, 2].astype(F32) + x_in[t, 1, 1].astype(F32)
        high = acc[t, rows_of(x, 1), :] + x_in[t, 0, 1].astype(F32) + x_in[t, 1, 2].astype(F32)
        total = jnp.concatenate([low, high], axis=0)
        unit = 1.0 / (128.0 * math.sqrt(D))
        gate = total[:, :wide] * (gs_ref[t].astype(F32) * unit)
        up = total[:, wide:] * (us_ref[t].astype(F32) * unit)
        hidden = (gate / (1.0 + jnp.exp(-gate)) * up).astype(BF16)
        rot[t] = jnp.dot(hidden, had[...], preferred_element_type=F32)

    def step(s, carry):
        pl.when(s < TILES)(lambda: stage_a(s))
        pl.when(jnp.logical_and(s >= LAG_B, s < TILES + LAG_B))(lambda: stage_b(s - LAG_B))
        pl.when(jnp.logical_and(s >= LAG_C, s < TILES + LAG_C))(lambda: stage_c(s - LAG_C))
        pl.when(s >= LAG_D)(lambda: stage_d(s - LAG_D))
        return carry

    lax.fori_loop(0, TILES + LAG_D, step, 0)

    for rows in range(0, OWN, 16):
        mixed = walsh([rot[t, rows : rows + 16, :] for t in range(TILES)])
        flat = jnp.concatenate(mixed, axis=1).astype(BF16)
        for j in range(nt):
            z[j, rows : rows + 16, :] = flat[:, j * piece : (j + 1) * piece]

    def z_copy(j, slot):
        return remote(z.at[j], a.at[slot], z_ssem.at[j], z_rsem.at[slot], (dp, j))

    def z_send(k, carry):
        z_copy(peer(k), me).start()
        return carry

    def z_wait(k, carry):
        z_copy(me, peer(k)).wait_recv()
        return carry

    pl.semaphore_wait(plane_sem, len(along_z))
    lax.fori_loop(1, nt, z_send, 0)
    a[me] = z[me]
    lax.fori_loop(1, nt, z_wait, 0)

    for rows in range(0, OWN, 16):
        mixed = walsh([a[i, rows : rows + 16, :].astype(F32) for i in range(nt)])
        for j in range(nt):
            r[j, rows : rows + 16, :] = (mixed[j] * (1.0 / math.sqrt(ff))).astype(BF16)

    my_rows = pl.ds(pl.multiple_of(c * OWN, OWN), OWN)
    other_core = pl.ds(pl.multiple_of((1 - c) * OWN, OWN), OWN)

    def r_copy(j, slot):
        cols = pl.ds(pl.multiple_of(slot * piece, piece), piece)
        return remote(r.at[j], y.at[x, my_rows, cols], r_ssem.at[j], r_rsem.at[slot], (dp, j))

    def r_send(k, carry):
        r_copy(peer(k), me).start()
        return carry

    def r_wait(k, carry):
        r_copy(me, peer(k)).wait_recv()
        return carry

    lax.fori_loop(1, nt, r_send, 0)
    y[x, my_rows, pl.ds(pl.multiple_of(me * piece, piece), piece)] = r[me]
    lax.fori_loop(1, nt, r_wait, 0)

    half_rows = [pl.ds(pl.multiple_of(c * OWN + h * SUB, SUB), SUB) for h in range(2)]

    def ag(sem, chip, rows, device):
        return remote(y.at[chip, rows, :], y.at[chip, rows, :], ag_ssem.at[sem], ag_rsem.at[sem], device)

    ag(0, x, my_rows, dev_right).start()
    ag(1, x, my_rows, dev_left).start()
    ag(2, x, my_rows, dev_core).start()

    def rs_copy(chip, j, slot):
        return remote(
            part.at[chip, j], gathered.at[chip, slot], rs_ssem.at[chip, j], rs_rsem.at[chip, slot], (dp, j)
        )

    def down(chip):
        result = jnp.dot(y[chip], wd[...], preferred_element_type=F32)
        middle = result.shape[1] // 2
        for j in range(nt):
            rows = result[j * group : (j + 1) * group]
            part[chip, j] = jnp.concatenate([rows[:, :middle], rows[:, middle:]], axis=0).astype(BF16)

        def send(k, carry):
            rs_copy(chip, peer(k), me).start()
            return carry

        lax.fori_loop(1, nt, send, 0)
        gathered[chip, me] = part[chip, me]

    ag(2, x, other_core, dev_core).wait_recv()
    down(x)

    ag(0, left, my_rows, dev_right).wait_recv()
    ag(3, left, half_rows[0], dev_right).start()
    ag(4, left, my_rows, dev_core).start()
    ag(1, right, my_rows, dev_left).wait_recv()
    ag(5, right, half_rows[1], dev_left).start()
    ag(6, right, my_rows, dev_core).start()

    ag(4, left, other_core, dev_core).wait_recv()
    down(left)
    ag(6, right, other_core, dev_core).wait_recv()
    down(right)

    ag(3, across, half_rows[0], dev_right).wait_recv()
    ag(7, across, half_rows[0], dev_core).start()
    ag(5, across, half_rows[1], dev_left).wait_recv()
    ag(8, across, half_rows[1], dev_core).start()
    other_half = [pl.ds(pl.multiple_of((1 - c) * OWN + h * SUB, SUB), SUB) for h in range(2)]
    ag(7, across, other_half[0], dev_core).wait_recv()
    ag(8, across, other_half[1], dev_core).wait_recv()
    down(across)

    def rs_wait(n, carry):
        rs_copy(n // (nt - 1), me, peer(n % (nt - 1) + 1)).wait_recv()
        return carry

    lax.fori_loop(0, NX * (nt - 1), rs_wait, 0)
    scale = ds_ref[...].astype(F32) * (1.0 / (64.0 * math.sqrt(ff)))
    blocks = []
    for chip in range(NX):
        total = gathered[chip, 0].astype(F32)
        for i in range(1, nt):
            total = total + gathered[chip, i].astype(F32)
        blocks.append(jnp.concatenate([total[:group], total[group:]], axis=1) * scale)
    out_ref[...] = jnp.concatenate(blocks, axis=0).astype(BF16)

    def core_done(t, carry):
        core_copy(t).wait_send()
        for way in range(2):
            for kind in range(3):
                x_copy(t, way, kind).wait_send()
        return carry

    lax.fori_loop(0, TILES, core_done, 0)

    def peers_done(k, carry):
        z_copy(peer(k), me).wait_send()
        r_copy(peer(k), me).wait_send()
        return carry

    lax.fori_loop(1, nt, peers_done, 0)

    def rs_done(n, carry):
        rs_copy(n // (nt - 1), peer(n % (nt - 1) + 1), me).wait_send()
        return carry

    lax.fori_loop(0, NX * (nt - 1), rs_done, 0)
    ag(0, x, my_rows, dev_right).wait_send()
    ag(1, x, my_rows, dev_left).wait_send()
    ag(2, x, my_rows, dev_core).wait_send()
    ag(3, left, half_rows[0], dev_right).wait_send()
    ag(4, left, my_rows, dev_core).wait_send()
    ag(5, right, half_rows[1], dev_left).wait_send()
    ag(6, right, my_rows, dev_core).wait_send()
    ag(7, across, half_rows[0], dev_core).wait_send()
    ag(8, across, half_rows[1], dev_core).wait_send()


def body(tokens, gate_codes, up_codes, down_codes, gate_scale, up_scale, down_scale):
    nt = lax.axis_size("tensor")
    depth, units = gate_codes.shape
    width = down_codes.shape[1]
    wide = units // TILES
    piece = units // nt
    group = TOKENS // (NX * nt)
    dma = pltpu.SemaphoreType.DMA
    any_space = pl.BlockSpec(memory_space=pl.ANY)
    vmem = pl.BlockSpec(memory_space=pltpu.VMEM)
    return pl.pallas_call(
        functools.partial(kernel, nt, units * nt),
        out_shape=jax.ShapeDtypeStruct((TOKENS // nt, width), BF16),
        in_specs=[any_space] * 4 + [vmem] * 3,
        out_specs=vmem,
        scratch_shapes=[
            pltpu.VMEM((TOKENS, depth), BF16),
            pltpu.VMEM((TOKENS, depth), BF16),
            pltpu.VMEM((TILES, 2, depth, wide), jnp.int32),
            pltpu.VMEM((units, width), jnp.int32),
            pltpu.VMEM((depth, 2 * wide), BF16),
            pltpu.VMEM((units, width), BF16),
            pltpu.VMEM((wide, wide), BF16),
            pltpu.VMEM((TILES, TOKENS // 2, 2 * wide), BF16),
            pltpu.VMEM((TILES, TOKENS // 2, 2 * wide), BF16),
            pltpu.VMEM((TILES, TOKENS // 2, 2 * wide), F32),
            pltpu.VMEM((TILES, 2, 3, SUB, 2 * wide), BF16),
            pltpu.VMEM((TILES, 2, 3, SUB, 2 * wide), BF16),
            pltpu.VMEM((TILES, OWN, wide), F32),
            pltpu.VMEM((nt, OWN, piece), BF16),
            pltpu.VMEM((nt, OWN, piece), BF16),
            pltpu.VMEM((nt, OWN, piece), BF16),
            pltpu.VMEM((NX, 2 * OWN, units), BF16),
            pltpu.VMEM((NX, nt, 2 * group, width // 2), BF16),
            pltpu.VMEM((NX, nt, 2 * group, width // 2), BF16),
            dma((1,)),
            dma((TILES, 2)),
            dma((TILES,)),
            dma((TILES,)),
            dma((TILES,)),
            dma((TILES, 2, 3)),
            dma((TILES, 2, 3)),
            dma((nt,)),
            dma((nt,)),
            dma((nt,)),
            dma((nt,)),
            dma((9,)),
            dma((9,)),
            dma((NX, nt)),
            dma((NX, nt)),
            pltpu.SemaphoreType.REGULAR,
        ],
        compiler_params=pltpu.CompilerParams(
            collective_id=0, has_side_effects=True, vmem_limit_bytes=56 * 1024 * 1024
        ),
        cost_estimate=pl.CostEstimate(
            flops=2 * TOKENS * depth * 3 * units, bytes_accessed=12 * depth * units, transcendentals=OWN * units
        ),
    )(
        tokens, gate_codes, up_codes, down_codes,
        gate_scale.reshape(TILES, 1, wide), up_scale.reshape(TILES, 1, wide), down_scale.reshape(1, width),
    )


def solution(mesh):
    in_specs = (
        P(None, "dp"),
        P("dp", "tensor"),
        P("dp", "tensor"),
        P("tensor", "dp"),
        P("tensor"),
        P("tensor"),
        P("dp"),
    )
    return jax.shard_map(body, mesh=mesh, in_specs=in_specs, out_specs=P("tensor", "dp"), check_vma=False)
```

```python
import functools
import math

import jax
import jax.numpy as jnp
from jax import lax
from jax.experimental import pallas as pl
from jax.experimental.pallas import tpu as pltpu
from jax.sharding import PartitionSpec as P

D = 8192
FF = 32768
TOKENS = 512
NX = 4
OWN = TOKENS // (2 * NX)
CHUNKS = 2
PART = OWN // CHUNKS
TILES = 4
TURN = 256
UNITS = CHUNKS * TILES
UNITS = CHUNKS * TILES
MESH = pl.DeviceIdType.MESH
F32 = jnp.float32
BF16 = jnp.bfloat16


def remote(src, dst, send_sem, recv_sem, device):
    return pltpu.make_async_remote_copy(
        src_ref=src,
        dst_ref=dst,
        send_sem=send_sem,
        recv_sem=recv_sem,
        device_id=device,
        device_id_type=MESH,
    )


def walsh(parts):
    stride = 1
    while stride < len(parts):
        done = list(parts)
        for i in range(len(parts)):
            if i & stride == 0:
                done[i] = parts[i] + parts[i + stride]
                done[i + stride] = parts[i] - parts[i + stride]
        parts = done
        stride *= 2
    return parts


def signs(size):
    rows = lax.broadcasted_iota(jnp.int32, (size, size), 0)
    cols = lax.broadcasted_iota(jnp.int32, (size, size), 1)
    bits = jnp.bitwise_and(rows, cols)
    for shift in (8, 4, 2, 1):
        bits = jnp.bitwise_xor(bits, jnp.right_shift(bits, shift))
    return (1 - 2 * jnp.bitwise_and(bits, 1)).astype(F32).astype(BF16)


def kernel(
    nt, ff,
    tok_hbm, gate_hbm, up_hbm, down_hbm, gs_ref, us_ref, ds_ref,
    out_ref,
    tok_in, tok, codes, down_codes, wd, had,
    core_out, core_in, acc, x_out, x_in,
    z, a, r, y, part, gathered, final,
    tok_sem, code_sem, down_sem,
    core_ssem, core_rsem, x_ssem, x_rsem,
    z_ssem, z_rsem, r_ssem, r_rsem, ag_ssem, ag_rsem, rs_ssem, rs_rsem, plane_sem,
):
    dp = lax.axis_index("dp")
    me = lax.axis_index("tensor")
    x = dp // 2
    c = dp % 2
    right = lax.rem(x + 1, NX)
    left = lax.rem(x + NX - 1, NX)
    across = lax.rem(x + 2, NX)
    dev_core = (x * 2 + 1 - c, me)
    dev_right = (right * 2 + c, me)
    dev_left = (left * 2 + c, me)
    units = gate_hbm.shape[1]
    wide = units // TILES
    depth = gate_hbm.shape[0]
    group = TOKENS // (NX * nt * CHUNKS)
    piece = units // nt

    def peer(k):
        return lax.rem(me + k, nt)

    tok_copy = pltpu.make_async_copy(tok_hbm, tok_in, tok_sem.at[0])
    tok_copy.start()

    def code_copies(t):
        cols = pl.ds(t * wide, wide)
        return (
            pltpu.make_async_copy(gate_hbm.at[:, cols], codes.at[t, 0], code_sem.at[t, 0]),
            pltpu.make_async_copy(up_hbm.at[:, cols], codes.at[t, 1], code_sem.at[t, 1]),
        )

    def fetch(t):
        for copy in code_copies(t):
            copy.start()

    down_copy = pltpu.make_async_copy(down_hbm, down_codes, down_sem.at[0])
    fetch(0)

    barrier = pltpu.get_barrier_semaphore()
    side = math.isqrt(nt)
    row, col = me // side, me % side
    along_y = [(dp, row * side + lax.rem(col + k, side)) for k in range(1, side)]
    along_z = [(dp, lax.rem(row + k, side) * side + col) for k in range(1, side)]
    greeted = [dev_core, dev_right, dev_left] + along_y + along_z
    for device in greeted:
        pl.semaphore_signal(barrier, inc=1, device_id=device, device_id_type=MESH)

    tok_copy.wait()
    fetch(1)
    half_groups = nt // 2
    for half in range(2):
        for chip in range(NX):
            for q in range(CHUNKS):
                rows = []
                for j in range(half_groups):
                    first = (half * half_groups + j) * (TOKENS // nt) + (chip * CHUNKS + q) * group
                    span = max(16, group)
                    base = first // span * span
                    rows.append(tok_in[base : base + span, :].astype(F32)[first - base : first - base + group])
                start = lax.rem(half + c, 2) * (TOKENS // 2) + chip * OWN + q * PART
                tok[pl.ds(pl.multiple_of(start, PART), PART), :] = jnp.concatenate(rows, axis=0).astype(BF16)

    gate_cols = pl.ds(0, wide)
    up_cols = pl.ds(wide, wide)

    def core_copy(t):
        return remote(core_out.at[t], core_in.at[t], core_ssem.at[t], core_rsem.at[t], dev_core)

    def x_copy(u, way, kind):
        return remote(
            x_out.at[u, way, kind], x_in.at[u, way, kind], x_ssem.at[u, way, kind], x_rsem.at[u, way, kind],
            dev_right if way == 0 else dev_left,
        )

    def multiply(t):
        for copy in code_copies(t):
            copy.wait()
        if t + 2 < TILES:
            fetch(t + 2)
        elif t + 2 == TILES:
            down_copy.start()
        for side, cols in ((0, gate_cols), (1, up_cols)):
            weights = (codes[t, side] - 8).astype(F32).astype(BF16)
            product = jnp.dot(tok[...], weights, preferred_element_type=F32)
            acc[t, :, cols] = product[: TOKENS // 2]
            core_out[t, :, cols] = product[TOKENS // 2 :].astype(BF16)
        if t == 0:
            pl.semaphore_wait(barrier, len(greeted))
        core_copy(t).start()

    def convert_down(t):
        rows = pl.ds(t * (units // TILES), units // TILES)
        wd[rows, :] = (down_codes[rows, :] - 8).astype(F32).astype(BF16)

    def unit_rows(u, chip):
        return pl.ds(pl.multiple_of(chip * OWN + u // TILES * PART, PART), PART)

    def both(u, chip, cols):
        rows = unit_rows(u, chip)
        return acc[u % TILES, rows, cols] + core_in[u % TILES, rows, cols].astype(F32)

    def stage_b(u):
        if u < TILES:
            core_copy(u).wait()
        for kind, pieces in ((0, ((across, gate_cols), (across, up_cols))), (1, ((right, up_cols), (left, gate_cols)))):
            for way in range(2):
                x_out[u, way, kind] = both(u, *pieces[way]).astype(BF16)
                x_copy(u, way, kind).start()

    def stage_c(u):
        for way, (chip, cols) in enumerate(((right, gate_cols), (left, up_cols))):
            x_copy(u, way, 0).wait_recv()
            x_out[u, way, 2] = (both(u, chip, cols) + x_in[u, way, 0].astype(F32)).astype(BF16)
            x_copy(u, way, 2).start()

    def stage_d(q):
        unit = 1.0 / (128.0 * math.sqrt(D))
        stacked = []
        for u in range(q * TILES, (q + 1) * TILES):
            t = u % TILES
            for way in range(2):
                for kind in (1, 2):
                    x_copy(u, way, kind).wait_recv()
            gate = both(u, x, gate_cols) + x_in[u, 0, 2].astype(F32) + x_in[u, 1, 1].astype(F32)
            gate = gate * (gs_ref[t].astype(F32) * unit)
            up = both(u, x, up_cols) + x_in[u, 0, 1].astype(F32) + x_in[u, 1, 2].astype(F32)
            up = up * (us_ref[t].astype(F32) * unit)
            hidden = gate / (1.0 + jnp.exp(-gate)) * up
            for col in range(0, wide, TURN):
                stacked.append(hidden[:, col : col + TURN].astype(BF16))
        turned = jnp.dot(jnp.concatenate(stacked, axis=0), had[...], preferred_element_type=F32)
        mixed = walsh([turned[i * PART : (i + 1) * PART] for i in range(len(stacked))])
        flat = jnp.concatenate(mixed, axis=1).astype(BF16)
        for j in range(nt):
            z[q, j] = flat[:, j * piece : (j + 1) * piece]

    def z_copy(q, j, slot):
        return remote(z.at[q, j], a.at[q, slot], z_ssem.at[q, j], z_rsem.at[q, slot], (dp, j))

    def stage_e(q):
        if q == 0:
            pl.semaphore_wait(plane_sem, len(along_z))

        def send(k, carry):
            z_copy(q, peer(k), me).start()
            return carry

        lax.fori_loop(1, nt, send, 0)
        a[q, me] = z[q, me]

    def chunk_rows(core):
        return pl.ds(pl.multiple_of(core * PART, PART), PART)

    def r_copy(q, j, slot):
        cols = pl.ds(pl.multiple_of(slot * piece, piece), piece)
        return remote(r.at[q, j], y.at[q, x, chunk_rows(c), cols], r_ssem.at[q, j], r_rsem.at[q, slot], (dp, j))

    def stage_f(q):
        def wait(k, carry):
            z_copy(q, me, peer(k)).wait_recv()
            return carry

        lax.fori_loop(1, nt, wait, 0)
        for rows in range(0, PART, 16):
            mixed = walsh([a[q, i, rows : rows + 16, :].astype(F32) for i in range(nt)])
            for j in range(nt):
                r[q, j, rows : rows + 16, :] = (mixed[j] * (1.0 / math.sqrt(ff))).astype(BF16)

        def send(k, carry):
            r_copy(q, peer(k), me).start()
            return carry

        lax.fori_loop(1, nt, send, 0)
        y[q, x, chunk_rows(c), pl.ds(pl.multiple_of(me * piece, piece), piece)] = r[q, me]

        def sent(k, carry):
            z_copy(q, peer(k), me).wait_send()
            return carry

        lax.fori_loop(1, nt, sent, 0)

    def gather(q, n, core=None):
        core = c if core is None else core
        low = pl.ds(pl.multiple_of(core * PART, PART // 2), PART // 2)
        high = pl.ds(pl.multiple_of(core * PART + PART // 2, PART // 2), PART // 2)
        whole = chunk_rows(core)
        chip, rows, device = (
            (x, low, dev_right), (x, high, dev_right), (x, high, dev_left), (x, low, dev_left), (x, whole, dev_core),
            (left, low, dev_right), (right, high, dev_left),
            (left, whole, dev_core), (right, whole, dev_core), (across, low, dev_core), (across, high, dev_core),
        )[n]
        block = y.at[q, chip, rows, :]
        return remote(block, block, ag_ssem.at[q, n], ag_rsem.at[q, n], device)

    def arrived(q, n):
        low = pl.ds(pl.multiple_of(c * PART, PART // 2), PART // 2)
        high = pl.ds(pl.multiple_of(c * PART + PART // 2, PART // 2), PART // 2)
        places = {
            0: (left, low), 1: (left, high), 2: (right, high), 3: (right, low), 5: (across, low), 6: (across, high),
        }
        if n in places:
            chip, rows = places[n]
            block = y.at[q, chip, rows, :]
            remote(block, block, ag_ssem.at[q, n], ag_rsem.at[q, n], dev_core).wait_recv()
        else:
            gather(q, n, 1 - c).wait_recv()

    def gather_start(q):
        def wait(k, carry):
            r_copy(q, me, peer(k)).wait_recv()
            return carry

        lax.fori_loop(1, nt, wait, 0)
        for n in (0, 2, 1, 3, 4):
            gather(q, n).start()

    def gather_on(q, pairs):
        for come, go in pairs:
            arrived(q, come)
            if go is not None:
                gather(q, go).start()

    def rs_copy(q, pair, j, slot):
        return remote(
            part.at[q, pair, j], gathered.at[q, pair, slot], rs_ssem.at[q, pair, j], rs_rsem.at[q, pair, slot], (dp, j)
        )

    def down(q, pair):
        first, second = ((x, left), (right, across))[pair]
        rows_in = jnp.concatenate([y[q, first], y[q, second]], axis=0)
        result = jnp.dot(rows_in, wd[...], preferred_element_type=F32)
        middle = result.shape[1] // 2
        for j in range(nt):
            rows = jnp.concatenate(
                [result[j * group : (j + 1) * group], result[(nt + j) * group : (nt + j + 1) * group]], axis=0
            )
            part[q, pair, j] = jnp.concatenate([rows[:, :middle], rows[:, middle:]], axis=0).astype(BF16)

        def send(k, carry):
            rs_copy(q, pair, peer(k), me).start()
            return carry

        lax.fori_loop(1, nt, send, 0)
        gathered[q, pair, me] = part[q, pair, me]

    def total(q, pair):
        def wait(k, carry):
            rs_copy(q, pair, me, peer(k)).wait_recv()
            return carry

        lax.fori_loop(1, nt, wait, 0)
        both = gathered[q, pair, 0].astype(F32)
        for i in range(1, nt):
            both = both + gathered[q, pair, i].astype(F32)
        rows = jnp.concatenate([both[: 2 * group], both[2 * group :]], axis=1)
        first, second = ((x, left), (right, across))[pair]
        final[first, q] = rows[:group]
        final[second, q] = rows[group:]

    multiply(0)
    for device in along_z:
        pl.semaphore_signal(plane_sem, inc=1, device_id=device, device_id_type=MESH)
    multiply(1)
    stage_b(0)
    multiply(2)
    stage_b(1)
    multiply(3)
    stage_b(2)
    stage_c(0)
    had[...] = signs(TURN)
    stage_b(3)
    stage_c(1)
    down_copy.wait()
    convert_down(0)
    stage_c(2)
    convert_down(1)
    stage_c(3)
    for u in range(TILES, UNITS):
        stage_b(u)
    convert_down(2)
    convert_down(3)
    stage_d(0)
    stage_e(0)
    stage_c(4)
    stage_c(5)
    stage_c(6)
    stage_f(0)
    stage_c(7)
    stage_d(1)
    stage_e(1)
    gather_start(0)
    gather_on(0, ((0, 5), (2, 6)))
    stage_f(1)
    gather_on(0, ((1, 7), (3, 8), (4, None), (7, None)))
    down(0, 0)
    gather_on(0, ((5, 9), (6, 10), (8, None), (9, None), (10, None)))
    down(0, 1)
    gather_start(1)
    gather_on(1, ((0, 5), (2, 6)))
    total(0, 0)
    gather_on(1, ((1, 7), (3, 8), (4, None), (7, None)))
    down(1, 0)
    gather_on(1, ((5, 9), (6, 10), (8, None), (9, None), (10, None)))
    down(1, 1)

    def peers_sent(k, carry):
        for q in range(CHUNKS):
            r_copy(q, peer(k), me).wait_send()
            for pair in range(2):
                rs_copy(q, pair, peer(k), me).wait_send()
        return carry

    lax.fori_loop(1, nt, peers_sent, 0)
    for q in range(CHUNKS):
        for n in range(11):
            gather(q, n).wait_send()
    for u in range(UNITS):
        for way in range(2):
            for kind in range(3):
                x_copy(u, way, kind).wait_send()

    total(0, 1)
    total(1, 0)
    total(1, 1)
    scale = ds_ref[...].astype(F32) * (1.0 / (64.0 * math.sqrt(ff)))
    blocks = [final[chip, q] for chip in range(NX) for q in range(CHUNKS)]
    out_ref[...] = (jnp.concatenate(blocks, axis=0) * scale).astype(BF16)


def body(tokens, gate_codes, up_codes, down_codes, gate_scale, up_scale, down_scale):
    nt = lax.axis_size("tensor")
    depth, units = gate_codes.shape
    width = down_codes.shape[1]
    wide = units // TILES
    piece = units // nt
    group = TOKENS // (NX * nt * CHUNKS)
    dma = pltpu.SemaphoreType.DMA
    any_space = pl.BlockSpec(memory_space=pl.ANY)
    vmem = pl.BlockSpec(memory_space=pltpu.VMEM)
    return pl.pallas_call(
        functools.partial(kernel, nt, units * nt),
        out_shape=jax.ShapeDtypeStruct((TOKENS // nt, width), BF16),
        in_specs=[any_space] * 4 + [vmem] * 3,
        out_specs=vmem,
        scratch_shapes=[
            pltpu.VMEM((TOKENS, depth), BF16),
            pltpu.VMEM((TOKENS, depth), BF16),
            pltpu.VMEM((TILES, 2, depth, wide), jnp.int32),
            pltpu.VMEM((units, width), jnp.int32),
            pltpu.VMEM((units, width), BF16),
            pltpu.VMEM((TURN, TURN), BF16),
            pltpu.VMEM((TILES, TOKENS // 2, 2 * wide), BF16),
            pltpu.VMEM((TILES, TOKENS // 2, 2 * wide), BF16),
            pltpu.VMEM((TILES, TOKENS // 2, 2 * wide), F32),
            pltpu.VMEM((UNITS, 2, 3, PART, wide), BF16),
            pltpu.VMEM((UNITS, 2, 3, PART, wide), BF16),
            pltpu.VMEM((CHUNKS, nt, PART, piece), BF16),
            pltpu.VMEM((CHUNKS, nt, PART, piece), BF16),
            pltpu.VMEM((CHUNKS, nt, PART, piece), BF16),
            pltpu.VMEM((CHUNKS, NX, 2 * PART, units), BF16),
            pltpu.VMEM((CHUNKS, 2, nt, 4 * group, width // 2), BF16),
            pltpu.VMEM((CHUNKS, 2, nt, 4 * group, width // 2), BF16),
            pltpu.VMEM((NX, CHUNKS, group, width), F32),
            dma((1,)),
            dma((TILES, 2)),
            dma((1,)),
            dma((TILES,)),
            dma((TILES,)),
            dma((UNITS, 2, 3)),
            dma((UNITS, 2, 3)),
            dma((CHUNKS, nt)),
            dma((CHUNKS, nt)),
            dma((CHUNKS, nt)),
            dma((CHUNKS, nt)),
            dma((CHUNKS, 11)),
            dma((CHUNKS, 11)),
            dma((CHUNKS, 2, nt)),
            dma((CHUNKS, 2, nt)),
            pltpu.SemaphoreType.REGULAR,
        ],
        compiler_params=pltpu.CompilerParams(
            collective_id=0, has_side_effects=True, vmem_limit_bytes=56 * 1024 * 1024
        ),
        cost_estimate=pl.CostEstimate(
            flops=2 * TOKENS * depth * 3 * units, bytes_accessed=12 * depth * units, transcendentals=OWN * units
        ),
    )(
        tokens, gate_codes, up_codes, down_codes,
        gate_scale.reshape(TILES, 1, wide), up_scale.reshape(TILES, 1, wide), down_scale.reshape(1, width),
    )


def solution(mesh):
    in_specs = (
        P(None, "dp"),
        P("dp", "tensor"),
        P("dp", "tensor"),
        P("tensor", "dp"),
        P("tensor"),
        P("tensor"),
        P("dp"),
    )
    return jax.shard_map(body, mesh=mesh, in_specs=in_specs, out_specs=P("tensor", "dp"), check_vma=False)
```

```python
import functools
import math

import jax
import jax.numpy as jnp
from jax import lax
from jax.experimental import pallas as pl
from jax.experimental.pallas import tpu as pltpu
from jax.sharding import PartitionSpec as P

D = 8192
FF = 32768
TOKENS = 512
NX = 4
OWN = TOKENS // (2 * NX)
CHUNKS = 2
PART = OWN // CHUNKS
TILES = 4
TURN = 256
UNITS = CHUNKS * TILES
UNITS = CHUNKS * TILES
MESH = pl.DeviceIdType.MESH
F32 = jnp.float32
BF16 = jnp.bfloat16


def remote(src, dst, send_sem, recv_sem, device):
    return pltpu.make_async_remote_copy(
        src_ref=src,
        dst_ref=dst,
        send_sem=send_sem,
        recv_sem=recv_sem,
        device_id=device,
        device_id_type=MESH,
    )


def unrolled(low, high, step, carry):
    for k in range(low, high):
        carry = step(k, carry)
    return carry


def walsh(parts):
    stride = 1
    while stride < len(parts):
        done = list(parts)
        for i in range(len(parts)):
            if i & stride == 0:
                done[i] = parts[i] + parts[i + stride]
                done[i + stride] = parts[i] - parts[i + stride]
        parts = done
        stride *= 2
    return parts


def signs(size):
    rows = lax.broadcasted_iota(jnp.int32, (size, size), 0)
    cols = lax.broadcasted_iota(jnp.int32, (size, size), 1)
    bits = jnp.bitwise_and(rows, cols)
    for shift in (8, 4, 2, 1):
        bits = jnp.bitwise_xor(bits, jnp.right_shift(bits, shift))
    return (1 - 2 * jnp.bitwise_and(bits, 1)).astype(F32).astype(BF16)


def kernel(
    nt, ff,
    tok_hbm, gate_hbm, up_hbm, down_hbm, gs_ref, us_ref, ds_ref,
    out_ref,
    tok_in, tok, codes, down_codes, wd, had,
    core_out, core_in, acc, x_out, x_in,
    z, a, r, y, part, gathered, final,
    tok_sem, code_sem, down_sem,
    core_ssem, core_rsem, x_ssem, x_rsem,
    z_ssem, z_rsem, r_ssem, r_rsem, ag_ssem, ag_rsem, rs_ssem, rs_rsem, plane_sem,
):
    dp = lax.axis_index("dp")
    me = lax.axis_index("tensor")
    x = dp // 2
    c = dp % 2
    right = lax.rem(x + 1, NX)
    left = lax.rem(x + NX - 1, NX)
    across = lax.rem(x + 2, NX)
    dev_core = (x * 2 + 1 - c, me)
    dev_right = (right * 2 + c, me)
    dev_left = (left * 2 + c, me)
    units = gate_hbm.shape[1]
    wide = units // TILES
    depth = gate_hbm.shape[0]
    group = TOKENS // (NX * nt * CHUNKS)
    piece = units // nt

    def peer(k):
        return lax.rem(me + k, nt)

    tok_copy = pltpu.make_async_copy(tok_hbm, tok_in, tok_sem.at[0])
    tok_copy.start()

    def code_copies(t):
        cols = pl.ds(t * wide, wide)
        return (
            pltpu.make_async_copy(gate_hbm.at[:, cols], codes.at[t, 0], code_sem.at[t, 0]),
            pltpu.make_async_copy(up_hbm.at[:, cols], codes.at[t, 1], code_sem.at[t, 1]),
        )

    def fetch(t):
        for copy in code_copies(t):
            copy.start()

    down_copy = pltpu.make_async_copy(down_hbm, down_codes, down_sem.at[0])
    fetch(0)

    barrier = pltpu.get_barrier_semaphore()
    side = math.isqrt(nt)
    row, col = me // side, me % side
    along_y = [(dp, row * side + lax.rem(col + k, side)) for k in range(1, side)]
    along_z = [(dp, lax.rem(row + k, side) * side + col) for k in range(1, side)]
    greeted = [dev_core, dev_right, dev_left] + along_y + along_z
    for device in greeted:
        pl.semaphore_signal(barrier, inc=1, device_id=device, device_id_type=MESH)

    tok_copy.wait()
    fetch(1)
    half_groups = nt // 2
    for half in range(2):
        for chip in range(NX):
            for q in range(CHUNKS):
                rows = []
                for j in range(half_groups):
                    first = (half * half_groups + j) * (TOKENS // nt) + (chip * CHUNKS + q) * group
                    span = max(16, group)
                    base = first // span * span
                    rows.append(tok_in[base : base + span, :].astype(F32)[first - base : first - base + group])
                start = lax.rem(half + c, 2) * (TOKENS // 2) + chip * OWN + q * PART
                tok[pl.ds(pl.multiple_of(start, PART), PART), :] = jnp.concatenate(rows, axis=0).astype(BF16)

    gate_cols = pl.ds(0, wide)
    up_cols = pl.ds(wide, wide)

    def core_copy(t):
        return remote(core_out.at[t], core_in.at[t], core_ssem.at[t], core_rsem.at[t], dev_core)

    def x_copy(u, way, kind):
        return remote(
            x_out.at[u, way, kind], x_in.at[u, way, kind], x_ssem.at[u, way, kind], x_rsem.at[u, way, kind],
            dev_right if way == 0 else dev_left,
        )

    def multiply(t):
        for copy in code_copies(t):
            copy.wait()
        if t + 2 < TILES:
            fetch(t + 2)
        elif t + 1 == TILES:
            down_copy.start()
        for side, cols in ((0, gate_cols), (1, up_cols)):
            weights = (codes[t, side] - 8).astype(F32).astype(BF16)
            product = jnp.dot(tok[...], weights, preferred_element_type=F32)
            acc[t, :, cols] = product[: TOKENS // 2]
            core_out[t, :, cols] = product[TOKENS // 2 :].astype(BF16)
        if t == 0:
            pl.semaphore_wait(barrier, len(greeted))
        core_copy(t).start()

    def convert_down(t):
        rows = pl.ds(t * (units // TILES), units // TILES)
        wd[rows, :] = (down_codes[rows, :] - 8).astype(F32).astype(BF16)

    def unit_rows(u, chip):
        return pl.ds(pl.multiple_of(chip * OWN + u // TILES * PART, PART), PART)

    def both(u, chip, cols):
        rows = unit_rows(u, chip)
        return acc[u % TILES, rows, cols] + core_in[u % TILES, rows, cols].astype(F32)

    def stage_b(u):
        if u < TILES:
            core_copy(u).wait()
        for kind, pieces in ((0, ((across, gate_cols), (across, up_cols))), (1, ((right, up_cols), (left, gate_cols)))):
            for way in range(2):
                x_out[u, way, kind] = both(u, *pieces[way]).astype(BF16)
                x_copy(u, way, kind).start()

    def stage_c(u):
        for way, (chip, cols) in enumerate(((right, gate_cols), (left, up_cols))):
            x_copy(u, way, 0).wait_recv()
            x_out[u, way, 2] = (both(u, chip, cols) + x_in[u, way, 0].astype(F32)).astype(BF16)
            x_copy(u, way, 2).start()

    def stage_d(q):
        unit = 1.0 / (128.0 * math.sqrt(D))
        stacked = []
        for u in range(q * TILES, (q + 1) * TILES):
            t = u % TILES
            for way in range(2):
                for kind in (1, 2):
                    x_copy(u, way, kind).wait_recv()
            gate = both(u, x, gate_cols) + x_in[u, 0, 2].astype(F32) + x_in[u, 1, 1].astype(F32)
            gate = gate * (gs_ref[t].astype(F32) * unit)
            up = both(u, x, up_cols) + x_in[u, 0, 1].astype(F32) + x_in[u, 1, 2].astype(F32)
            up = up * (us_ref[t].astype(F32) * unit)
            hidden = gate / (1.0 + jnp.exp(-gate)) * up
            for col in range(0, wide, TURN):
                stacked.append(hidden[:, col : col + TURN].astype(BF16))
        turned = jnp.dot(jnp.concatenate(stacked, axis=0), had[...], preferred_element_type=F32)
        mixed = walsh([turned[i * PART : (i + 1) * PART] for i in range(len(stacked))])
        flat = jnp.concatenate(mixed, axis=1).astype(BF16)
        for j in range(nt):
            z[q, j] = flat[:, j * piece : (j + 1) * piece]

    def z_copy(q, j, slot):
        return remote(z.at[q, j], a.at[q, slot], z_ssem.at[q, j], z_rsem.at[q, slot], (dp, j))

    def stage_e(q):
        if q == 0:
            pl.semaphore_wait(plane_sem, len(along_z))

        def send(k, carry):
            z_copy(q, peer(k), me).start()
            return carry

        unrolled(1, nt, send, 0)
        a[q, me] = z[q, me]

    def chunk_rows(core):
        return pl.ds(pl.multiple_of(core * PART, PART), PART)

    def r_copy(q, j, slot):
        cols = pl.ds(pl.multiple_of(slot * piece, piece), piece)
        return remote(r.at[q, j], y.at[q, x, chunk_rows(c), cols], r_ssem.at[q, j], r_rsem.at[q, slot], (dp, j))

    def stage_f(q):
        def wait(k, carry):
            z_copy(q, me, peer(k)).wait_recv()
            return carry

        unrolled(1, nt, wait, 0)
        for rows in range(0, PART, 16):
            mixed = walsh([a[q, i, rows : rows + 16, :].astype(F32) for i in range(nt)])
            for j in range(nt):
                r[q, j, rows : rows + 16, :] = (mixed[j] * (1.0 / math.sqrt(ff))).astype(BF16)

        def send(k, carry):
            r_copy(q, peer(k), me).start()
            return carry

        unrolled(1, nt, send, 0)
        y[q, x, chunk_rows(c), pl.ds(pl.multiple_of(me * piece, piece), piece)] = r[q, me]

        def sent(k, carry):
            z_copy(q, peer(k), me).wait_send()
            return carry

        unrolled(1, nt, sent, 0)

    def gather(q, n, core=None):
        core = c if core is None else core
        low = pl.ds(pl.multiple_of(core * PART, PART // 2), PART // 2)
        high = pl.ds(pl.multiple_of(core * PART + PART // 2, PART // 2), PART // 2)
        whole = chunk_rows(core)
        chip, rows, device = (
            (x, low, dev_right), (x, high, dev_right), (x, high, dev_left), (x, low, dev_left), (x, whole, dev_core),
            (left, low, dev_right), (right, high, dev_left),
            (left, whole, dev_core), (right, whole, dev_core), (across, low, dev_core), (across, high, dev_core),
        )[n]
        block = y.at[q, chip, rows, :]
        return remote(block, block, ag_ssem.at[q, n], ag_rsem.at[q, n], device)

    def arrived(q, n):
        low = pl.ds(pl.multiple_of(c * PART, PART // 2), PART // 2)
        high = pl.ds(pl.multiple_of(c * PART + PART // 2, PART // 2), PART // 2)
        places = {
            0: (left, low), 1: (left, high), 2: (right, high), 3: (right, low), 5: (across, low), 6: (across, high),
        }
        if n in places:
            chip, rows = places[n]
            block = y.at[q, chip, rows, :]
            remote(block, block, ag_ssem.at[q, n], ag_rsem.at[q, n], dev_core).wait_recv()
        else:
            gather(q, n, 1 - c).wait_recv()

    def gather_start(q):
        def wait(k, carry):
            r_copy(q, me, peer(k)).wait_recv()
            return carry

        unrolled(1, nt, wait, 0)
        for n in (0, 2, 1, 3, 4):
            gather(q, n).start()

    def gather_on(q, pairs):
        for come, go in pairs:
            arrived(q, come)
            if go is not None:
                gather(q, go).start()

    def rs_copy(q, pair, j, slot):
        return remote(
            part.at[q, pair, j], gathered.at[q, pair, slot], rs_ssem.at[q, pair, j], rs_rsem.at[q, pair, slot], (dp, j)
        )

    def down(q, pair):
        first, second = ((x, left), (right, across))[pair]
        rows_in = jnp.concatenate([y[q, first], y[q, second]], axis=0)
        result = jnp.dot(rows_in, wd[...], preferred_element_type=F32)
        middle = result.shape[1] // 2
        for j in range(nt):
            rows = jnp.concatenate(
                [result[j * group : (j + 1) * group], result[(nt + j) * group : (nt + j + 1) * group]], axis=0
            )
            part[q, pair, j] = jnp.concatenate([rows[:, :middle], rows[:, middle:]], axis=0).astype(BF16)

        def send(k, carry):
            rs_copy(q, pair, peer(k), me).start()
            return carry

        unrolled(1, nt, send, 0)
        gathered[q, pair, me] = part[q, pair, me]

    def total(q, pair):
        def wait(k, carry):
            rs_copy(q, pair, me, peer(k)).wait_recv()
            return carry

        unrolled(1, nt, wait, 0)
        both = gathered[q, pair, 0].astype(F32)
        for i in range(1, nt):
            both = both + gathered[q, pair, i].astype(F32)
        rows = jnp.concatenate([both[: 2 * group], both[2 * group :]], axis=1)
        first, second = ((x, left), (right, across))[pair]
        final[first, q] = rows[:group]
        final[second, q] = rows[group:]

    multiply(0)
    for device in along_z:
        pl.semaphore_signal(plane_sem, inc=1, device_id=device, device_id_type=MESH)
    multiply(1)
    stage_b(0)
    multiply(2)
    stage_b(1)
    multiply(3)
    stage_b(2)
    stage_c(0)
    stage_b(3)
    stage_c(1)
    had[...] = signs(TURN)
    stage_c(2)
    stage_c(3)
    for u in range(TILES, UNITS):
        stage_b(u)
    stage_d(0)
    stage_e(0)
    stage_c(4)
    down_copy.wait()
    convert_down(0)
    stage_c(5)
    convert_down(1)
    stage_c(6)
    convert_down(2)
    convert_down(3)
    stage_f(0)
    stage_c(7)
    stage_d(1)
    stage_e(1)
    gather_start(0)
    stage_f(1)
    gather_on(0, ((0, 5), (2, 6), (1, 7), (3, 8), (4, None), (7, None)))
    down(0, 0)
    gather_start(1)
    gather_on(0, ((5, 9), (6, 10), (8, None), (9, None), (10, None)))
    down(0, 1)
    gather_on(1, ((0, 5), (2, 6), (1, 7), (3, 8), (4, None), (7, None)))
    down(1, 0)
    total(0, 0)
    gather_on(1, ((5, 9), (6, 10), (8, None), (9, None), (10, None)))
    down(1, 1)

    def peers_sent(k, carry):
        for q in range(CHUNKS):
            r_copy(q, peer(k), me).wait_send()
            for pair in range(2):
                rs_copy(q, pair, peer(k), me).wait_send()
        return carry

    unrolled(1, nt, peers_sent, 0)
    for q in range(CHUNKS):
        for n in range(11):
            gather(q, n).wait_send()
    for u in range(UNITS):
        for way in range(2):
            for kind in range(3):
                x_copy(u, way, kind).wait_send()

    total(0, 1)
    total(1, 0)
    total(1, 1)
    scale = ds_ref[...].astype(F32) * (1.0 / (64.0 * math.sqrt(ff)))
    blocks = [final[chip, q] for chip in range(NX) for q in range(CHUNKS)]
    out_ref[...] = (jnp.concatenate(blocks, axis=0) * scale).astype(BF16)


def body(tokens, gate_codes, up_codes, down_codes, gate_scale, up_scale, down_scale):
    nt = lax.axis_size("tensor")
    depth, units = gate_codes.shape
    width = down_codes.shape[1]
    wide = units // TILES
    piece = units // nt
    group = TOKENS // (NX * nt * CHUNKS)
    dma = pltpu.SemaphoreType.DMA
    any_space = pl.BlockSpec(memory_space=pl.ANY)
    vmem = pl.BlockSpec(memory_space=pltpu.VMEM)
    return pl.pallas_call(
        functools.partial(kernel, nt, units * nt),
        out_shape=jax.ShapeDtypeStruct((TOKENS // nt, width), BF16),
        in_specs=[any_space] * 4 + [vmem] * 3,
        out_specs=vmem,
        scratch_shapes=[
            pltpu.VMEM((TOKENS, depth), BF16),
            pltpu.VMEM((TOKENS, depth), BF16),
            pltpu.VMEM((TILES, 2, depth, wide), jnp.int32),
            pltpu.VMEM((units, width), jnp.int32),
            pltpu.VMEM((units, width), BF16),
            pltpu.VMEM((TURN, TURN), BF16),
            pltpu.VMEM((TILES, TOKENS // 2, 2 * wide), BF16),
            pltpu.VMEM((TILES, TOKENS // 2, 2 * wide), BF16),
            pltpu.VMEM((TILES, TOKENS // 2, 2 * wide), F32),
            pltpu.VMEM((UNITS, 2, 3, PART, wide), BF16),
            pltpu.VMEM((UNITS, 2, 3, PART, wide), BF16),
            pltpu.VMEM((CHUNKS, nt, PART, piece), BF16),
            pltpu.VMEM((CHUNKS, nt, PART, piece), BF16),
            pltpu.VMEM((CHUNKS, nt, PART, piece), BF16),
            pltpu.VMEM((CHUNKS, NX, 2 * PART, units), BF16),
            pltpu.VMEM((CHUNKS, 2, nt, 4 * group, width // 2), BF16),
            pltpu.VMEM((CHUNKS, 2, nt, 4 * group, width // 2), BF16),
            pltpu.VMEM((NX, CHUNKS, group, width), F32),
            dma((1,)),
            dma((TILES, 2)),
            dma((1,)),
            dma((TILES,)),
            dma((TILES,)),
            dma((UNITS, 2, 3)),
            dma((UNITS, 2, 3)),
            dma((CHUNKS, nt)),
            dma((CHUNKS, nt)),
            dma((CHUNKS, nt)),
            dma((CHUNKS, nt)),
            dma((CHUNKS, 11)),
            dma((CHUNKS, 11)),
            dma((CHUNKS, 2, nt)),
            dma((CHUNKS, 2, nt)),
            pltpu.SemaphoreType.REGULAR,
        ],
        compiler_params=pltpu.CompilerParams(
            collective_id=0, has_side_effects=True, vmem_limit_bytes=56 * 1024 * 1024
        ),
        cost_estimate=pl.CostEstimate(
            flops=2 * TOKENS * depth * 3 * units, bytes_accessed=12 * depth * units, transcendentals=OWN * units
        ),
    )(
        tokens, gate_codes, up_codes, down_codes,
        gate_scale.reshape(TILES, 1, wide), up_scale.reshape(TILES, 1, wide), down_scale.reshape(1, width),
    )


def solution(mesh):
    in_specs = (
        P(None, "dp"),
        P("dp", "tensor"),
        P("dp", "tensor"),
        P("tensor", "dp"),
        P("tensor"),
        P("tensor"),
        P("dp"),
    )
    return jax.shard_map(body, mesh=mesh, in_specs=in_specs, out_specs=P("tensor", "dp"), check_vma=False)
```

```python
import functools
import math

import jax
import jax.numpy as jnp
from jax import lax
from jax.experimental import pallas as pl
from jax.experimental.pallas import tpu as pltpu
from jax.sharding import PartitionSpec as P

D = 8192
FF = 32768
TOKENS = 512
NX = 4
OWN = TOKENS // (2 * NX)
CHUNKS = 2
PART = OWN // CHUNKS
TILES = 4
TURN = 256
UNITS = CHUNKS * TILES
UNITS = CHUNKS * TILES
MESH = pl.DeviceIdType.MESH
F32 = jnp.float32
BF16 = jnp.bfloat16


def remote(src, dst, send_sem, recv_sem, device):
    return pltpu.make_async_remote_copy(
        src_ref=src,
        dst_ref=dst,
        send_sem=send_sem,
        recv_sem=recv_sem,
        device_id=device,
        device_id_type=MESH,
    )


def unrolled(low, high, step, carry):
    for k in range(low, high):
        carry = step(k, carry)
    return carry


def walsh(parts):
    stride = 1
    while stride < len(parts):
        done = list(parts)
        for i in range(len(parts)):
            if i & stride == 0:
                done[i] = parts[i] + parts[i + stride]
                done[i + stride] = parts[i] - parts[i + stride]
        parts = done
        stride *= 2
    return parts


def signs(size):
    rows = lax.broadcasted_iota(jnp.int32, (size, size), 0)
    cols = lax.broadcasted_iota(jnp.int32, (size, size), 1)
    bits = jnp.bitwise_and(rows, cols)
    for shift in (8, 4, 2, 1):
        bits = jnp.bitwise_xor(bits, jnp.right_shift(bits, shift))
    return (1 - 2 * jnp.bitwise_and(bits, 1)).astype(F32).astype(BF16)


def kernel(
    nt, ff,
    tok_hbm, gate_hbm, up_hbm, down_hbm, gs_ref, us_ref, ds_ref,
    out_ref,
    tok_in, tok, codes, down_codes, wd, had,
    core_out, core_in, acc, x_out, x_in,
    z, a, r, y, part, gathered, final,
    tok_sem, code_sem, down_sem,
    core_ssem, core_rsem, x_ssem, x_rsem,
    z_ssem, z_rsem, r_ssem, r_rsem, ag_ssem, ag_rsem, rs_ssem, rs_rsem, plane_sem,
):
    dp = lax.axis_index("dp")
    me = lax.axis_index("tensor")
    x = dp // 2
    c = dp % 2
    right = lax.rem(x + 1, NX)
    left = lax.rem(x + NX - 1, NX)
    across = lax.rem(x + 2, NX)
    dev_core = (x * 2 + 1 - c, me)
    dev_right = (right * 2 + c, me)
    dev_left = (left * 2 + c, me)
    units = gate_hbm.shape[1]
    wide = units // TILES
    depth = gate_hbm.shape[0]
    group = TOKENS // (NX * nt * CHUNKS)
    piece = units // nt

    def peer(k):
        return lax.rem(me + k, nt)

    tok_copy = pltpu.make_async_copy(tok_hbm, tok_in, tok_sem.at[0])
    tok_copy.start()

    def code_copies(t):
        cols = pl.ds(t * wide, wide)
        return (
            pltpu.make_async_copy(gate_hbm.at[:, cols], codes.at[t, 0], code_sem.at[t, 0]),
            pltpu.make_async_copy(up_hbm.at[:, cols], codes.at[t, 1], code_sem.at[t, 1]),
        )

    def fetch(t):
        for copy in code_copies(t):
            copy.start()

    down_copy = pltpu.make_async_copy(down_hbm, down_codes, down_sem.at[0])
    fetch(0)

    barrier = pltpu.get_barrier_semaphore()
    side = math.isqrt(nt)
    row, col = me // side, me % side
    along_y = [(dp, row * side + lax.rem(col + k, side)) for k in range(1, side)]
    along_z = [(dp, lax.rem(row + k, side) * side + col) for k in range(1, side)]
    greeted = [dev_core, dev_right, dev_left] + along_y + along_z
    for device in greeted:
        pl.semaphore_signal(barrier, inc=1, device_id=device, device_id_type=MESH)

    tok_copy.wait()
    fetch(1)
    half_groups = nt // 2
    for half in range(2):
        for chip in range(NX):
            for q in range(CHUNKS):
                rows = []
                for j in range(half_groups):
                    first = (half * half_groups + j) * (TOKENS // nt) + (chip * CHUNKS + q) * group
                    span = max(16, group)
                    base = first // span * span
                    rows.append(tok_in[base : base + span, :].astype(F32)[first - base : first - base + group])
                start = lax.rem(half + c, 2) * (TOKENS // 2) + chip * OWN + q * PART
                tok[pl.ds(pl.multiple_of(start, PART), PART), :] = jnp.concatenate(rows, axis=0).astype(BF16)

    gate_cols = pl.ds(0, wide)
    up_cols = pl.ds(wide, wide)

    def core_copy(t):
        return remote(core_out.at[t], core_in.at[t], core_ssem.at[t], core_rsem.at[t], dev_core)

    def x_copy(u, way, kind):
        return remote(
            x_out.at[u, way, kind], x_in.at[u, way, kind], x_ssem.at[u, way, kind], x_rsem.at[u, way, kind],
            dev_right if way == 0 else dev_left,
        )

    def multiply(t):
        for copy in code_copies(t):
            copy.wait()
        if t + 2 < TILES:
            fetch(t + 2)
        elif t + 1 == TILES:
            down_copy.start()
        for side, cols in ((0, gate_cols), (1, up_cols)):
            weights = (codes[t, side] - 8).astype(F32).astype(BF16)
            product = jnp.dot(tok[...], weights, preferred_element_type=F32)
            acc[t, :, cols] = product[: TOKENS // 2]
            core_out[t, :, cols] = product[TOKENS // 2 :].astype(BF16)
        if t == 0:
            pl.semaphore_wait(barrier, len(greeted))
        core_copy(t).start()

    def convert_down(t):
        rows = pl.ds(t * (units // TILES), units // TILES)
        wd[rows, :] = (down_codes[rows, :] - 8).astype(F32).astype(BF16)

    def unit_rows(u, chip):
        return pl.ds(pl.multiple_of(chip * OWN + u // TILES * PART, PART), PART)

    def both(u, chip, cols):
        rows = unit_rows(u, chip)
        return acc[u % TILES, rows, cols] + core_in[u % TILES, rows, cols].astype(F32)

    def stage_b(u):
        if u < TILES:
            core_copy(u).wait()
        for kind, pieces in ((0, ((across, gate_cols), (across, up_cols))), (1, ((right, up_cols), (left, gate_cols)))):
            for way in range(2):
                x_out[u, way, kind] = both(u, *pieces[way]).astype(BF16)
                x_copy(u, way, kind).start()

    def stage_c(u):
        for way, (chip, cols) in enumerate(((right, gate_cols), (left, up_cols))):
            x_copy(u, way, 0).wait_recv()
            x_out[u, way, 2] = (both(u, chip, cols) + x_in[u, way, 0].astype(F32)).astype(BF16)
            x_copy(u, way, 2).start()

    def stage_d(q):
        unit = 1.0 / (128.0 * math.sqrt(D))
        stacked = []
        for u in range(q * TILES, (q + 1) * TILES):
            t = u % TILES
            for way in range(2):
                for kind in (1, 2):
                    x_copy(u, way, kind).wait_recv()
            gate = both(u, x, gate_cols) + x_in[u, 0, 2].astype(F32) + x_in[u, 1, 1].astype(F32)
            gate = gate * (gs_ref[t].astype(F32) * unit)
            up = both(u, x, up_cols) + x_in[u, 0, 1].astype(F32) + x_in[u, 1, 2].astype(F32)
            up = up * (us_ref[t].astype(F32) * unit)
            hidden = gate / (1.0 + jnp.exp(-gate)) * up
            for col in range(0, wide, TURN):
                stacked.append(hidden[:, col : col + TURN].astype(BF16))
        turned = jnp.dot(jnp.concatenate(stacked, axis=0), had[...], preferred_element_type=F32)
        mixed = walsh([turned[i * PART : (i + 1) * PART] for i in range(len(stacked))])
        flat = jnp.concatenate(mixed, axis=1).astype(BF16)
        for j in range(nt):
            z[q, j] = flat[:, j * piece : (j + 1) * piece]

    def z_copy(q, j, slot):
        return remote(z.at[q, j], a.at[q, slot], z_ssem.at[q, j], z_rsem.at[q, slot], (dp, j))

    def stage_e(q):
        if q == 0:
            pl.semaphore_wait(plane_sem, len(along_z))

        def send(k, carry):
            z_copy(q, peer(k), me).start()
            return carry

        unrolled(1, nt, send, 0)
        a[q, me] = z[q, me]

    def chunk_rows(core):
        return pl.ds(pl.multiple_of(core * PART, PART), PART)

    def r_copy(q, j, slot):
        cols = pl.ds(pl.multiple_of(slot * piece, piece), piece)
        return remote(r.at[q, j], y.at[q, x, chunk_rows(c), cols], r_ssem.at[q, j], r_rsem.at[q, slot], (dp, j))

    def stage_f(q):
        def wait(k, carry):
            z_copy(q, me, peer(k)).wait_recv()
            return carry

        unrolled(1, nt, wait, 0)
        for rows in range(0, PART, 16):
            mixed = walsh([a[q, i, rows : rows + 16, :].astype(F32) for i in range(nt)])
            for j in range(nt):
                r[q, j, rows : rows + 16, :] = (mixed[j] * (1.0 / math.sqrt(ff))).astype(BF16)

        def send(k, carry):
            r_copy(q, peer(k), me).start()
            return carry

        unrolled(1, nt, send, 0)
        y[q, x, chunk_rows(c), pl.ds(pl.multiple_of(me * piece, piece), piece)] = r[q, me]

        def sent(k, carry):
            z_copy(q, peer(k), me).wait_send()
            return carry

        unrolled(1, nt, sent, 0)

    def gather(q, n, core=None):
        core = c if core is None else core
        low = pl.ds(pl.multiple_of(core * PART, PART // 2), PART // 2)
        high = pl.ds(pl.multiple_of(core * PART + PART // 2, PART // 2), PART // 2)
        whole = chunk_rows(core)
        chip, rows, device = (
            (x, low, dev_right), (x, high, dev_right), (x, high, dev_left), (x, low, dev_left), (x, whole, dev_core),
            (left, low, dev_right), (right, high, dev_left),
            (left, whole, dev_core), (right, whole, dev_core), (across, low, dev_core), (across, high, dev_core),
        )[n]
        block = y.at[q, chip, rows, :]
        return remote(block, block, ag_ssem.at[q, n], ag_rsem.at[q, n], device)

    def arrived(q, n):
        low = pl.ds(pl.multiple_of(c * PART, PART // 2), PART // 2)
        high = pl.ds(pl.multiple_of(c * PART + PART // 2, PART // 2), PART // 2)
        places = {
            0: (left, low), 1: (left, high), 2: (right, high), 3: (right, low), 5: (across, low), 6: (across, high),
        }
        if n in places:
            chip, rows = places[n]
            block = y.at[q, chip, rows, :]
            remote(block, block, ag_ssem.at[q, n], ag_rsem.at[q, n], dev_core).wait_recv()
        else:
            gather(q, n, 1 - c).wait_recv()

    def gather_start(q):
        def wait(k, carry):
            r_copy(q, me, peer(k)).wait_recv()
            return carry

        unrolled(1, nt, wait, 0)
        for n in (0, 2, 1, 3, 4):
            gather(q, n).start()

    def gather_on(q, pairs):
        for come, go in pairs:
            arrived(q, come)
            if go is not None:
                gather(q, go).start()

    def rs_copy(q, pair, j, slot):
        return remote(
            part.at[q, pair, j], gathered.at[q, pair, slot], rs_ssem.at[q, pair, j], rs_rsem.at[q, pair, slot], (dp, j)
        )

    def down(q, pair):
        first, second = ((x, left), (right, across))[pair]
        rows_in = jnp.concatenate([y[q, first], y[q, second]], axis=0)
        result = jnp.dot(rows_in, wd[...], preferred_element_type=F32)
        middle = result.shape[1] // 2
        for j in range(nt):
            rows = jnp.concatenate(
                [result[j * group : (j + 1) * group], result[(nt + j) * group : (nt + j + 1) * group]], axis=0
            )
            part[q, pair, j] = jnp.concatenate([rows[:, :middle], rows[:, middle:]], axis=0).astype(BF16)

        def send(k, carry):
            rs_copy(q, pair, peer(k), me).start()
            return carry

        unrolled(1, nt, send, 0)
        gathered[q, pair, me] = part[q, pair, me]

    def total(q, pair):
        def wait(k, carry):
            rs_copy(q, pair, me, peer(k)).wait_recv()
            return carry

        unrolled(1, nt, wait, 0)
        both = gathered[q, pair, 0].astype(F32)
        for i in range(1, nt):
            both = both + gathered[q, pair, i].astype(F32)
        rows = jnp.concatenate([both[: 2 * group], both[2 * group :]], axis=1)
        first, second = ((x, left), (right, across))[pair]
        final[first, q] = rows[:group]
        final[second, q] = rows[group:]

    multiply(0)
    for device in along_z:
        pl.semaphore_signal(plane_sem, inc=1, device_id=device, device_id_type=MESH)
    multiply(1)
    stage_b(0)
    multiply(2)
    stage_b(1)
    multiply(3)
    stage_b(2)
    stage_c(0)
    stage_b(3)
    stage_c(1)
    had[...] = signs(TURN)
    stage_c(2)
    stage_c(3)
    for u in range(TILES, UNITS):
        stage_b(u)
    stage_d(0)
    stage_e(0)
    stage_c(4)
    down_copy.wait()
    convert_down(0)
    stage_c(5)
    convert_down(1)
    stage_c(6)
    convert_down(2)
    convert_down(3)
    stage_c(7)
    stage_f(0)
    stage_d(1)
    stage_e(1)
    gather_start(0)
    stage_f(1)
    gather_on(0, ((0, 5), (2, 6), (1, 7), (3, 8), (4, None), (7, None)))
    down(0, 0)
    gather_start(1)
    gather_on(0, ((5, 9), (6, 10), (8, None), (9, None), (10, None)))
    down(0, 1)
    gather_on(1, ((0, 5), (2, 6), (1, 7), (3, 8), (4, None), (7, None)))
    down(1, 0)
    total(0, 0)
    gather_on(1, ((5, 9), (6, 10), (8, None), (9, None), (10, None)))
    down(1, 1)

    def peers_sent(k, carry):
        for q in range(CHUNKS):
            r_copy(q, peer(k), me).wait_send()
            for pair in range(2):
                rs_copy(q, pair, peer(k), me).wait_send()
        return carry

    unrolled(1, nt, peers_sent, 0)
    for q in range(CHUNKS):
        for n in range(11):
            gather(q, n).wait_send()
    for u in range(UNITS):
        for way in range(2):
            for kind in range(3):
                x_copy(u, way, kind).wait_send()

    total(0, 1)
    total(1, 0)
    total(1, 1)
    scale = ds_ref[...].astype(F32) * (1.0 / (64.0 * math.sqrt(ff)))
    blocks = [final[chip, q] for chip in range(NX) for q in range(CHUNKS)]
    out_ref[...] = (jnp.concatenate(blocks, axis=0) * scale).astype(BF16)


def body(tokens, gate_codes, up_codes, down_codes, gate_scale, up_scale, down_scale):
    nt = lax.axis_size("tensor")
    depth, units = gate_codes.shape
    width = down_codes.shape[1]
    wide = units // TILES
    piece = units // nt
    group = TOKENS // (NX * nt * CHUNKS)
    dma = pltpu.SemaphoreType.DMA
    any_space = pl.BlockSpec(memory_space=pl.ANY)
    vmem = pl.BlockSpec(memory_space=pltpu.VMEM)
    return pl.pallas_call(
        functools.partial(kernel, nt, units * nt),
        out_shape=jax.ShapeDtypeStruct((TOKENS // nt, width), BF16),
        in_specs=[any_space] * 4 + [vmem] * 3,
        out_specs=vmem,
        scratch_shapes=[
            pltpu.VMEM((TOKENS, depth), BF16),
            pltpu.VMEM((TOKENS, depth), BF16),
            pltpu.VMEM((TILES, 2, depth, wide), jnp.int32),
            pltpu.VMEM((units, width), jnp.int32),
            pltpu.VMEM((units, width), BF16),
            pltpu.VMEM((TURN, TURN), BF16),
            pltpu.VMEM((TILES, TOKENS // 2, 2 * wide), BF16),
            pltpu.VMEM((TILES, TOKENS // 2, 2 * wide), BF16),
            pltpu.VMEM((TILES, TOKENS // 2, 2 * wide), F32),
            pltpu.VMEM((UNITS, 2, 3, PART, wide), BF16),
            pltpu.VMEM((UNITS, 2, 3, PART, wide), BF16),
            pltpu.VMEM((CHUNKS, nt, PART, piece), BF16),
            pltpu.VMEM((CHUNKS, nt, PART, piece), BF16),
            pltpu.VMEM((CHUNKS, nt, PART, piece), BF16),
            pltpu.VMEM((CHUNKS, NX, 2 * PART, units), BF16),
            pltpu.VMEM((CHUNKS, 2, nt, 4 * group, width // 2), BF16),
            pltpu.VMEM((CHUNKS, 2, nt, 4 * group, width // 2), BF16),
            pltpu.VMEM((NX, CHUNKS, group, width), F32),
            dma((1,)),
            dma((TILES, 2)),
            dma((1,)),
            dma((TILES,)),
            dma((TILES,)),
            dma((UNITS, 2, 3)),
            dma((UNITS, 2, 3)),
            dma((CHUNKS, nt)),
            dma((CHUNKS, nt)),
            dma((CHUNKS, nt)),
            dma((CHUNKS, nt)),
            dma((CHUNKS, 11)),
            dma((CHUNKS, 11)),
            dma((CHUNKS, 2, nt)),
            dma((CHUNKS, 2, nt)),
            pltpu.SemaphoreType.REGULAR,
        ],
        compiler_params=pltpu.CompilerParams(
            collective_id=0, has_side_effects=True, vmem_limit_bytes=56 * 1024 * 1024
        ),
        cost_estimate=pl.CostEstimate(
            flops=2 * TOKENS * depth * 3 * units, bytes_accessed=12 * depth * units, transcendentals=OWN * units
        ),
    )(
        tokens, gate_codes, up_codes, down_codes,
        gate_scale.reshape(TILES, 1, wide), up_scale.reshape(TILES, 1, wide), down_scale.reshape(1, width),
    )


def solution(mesh):
    in_specs = (
        P(None, "dp"),
        P("dp", "tensor"),
        P("dp", "tensor"),
        P("tensor", "dp"),
        P("tensor"),
        P("tensor"),
        P("dp"),
    )
    return jax.shard_map(body, mesh=mesh, in_specs=in_specs, out_specs=P("tensor", "dp"), check_vma=False)
```
